256 devices in a mesh: dap: 128 (over y_lo, z, x, core), dp: 2 (over y_hi).
Axes of the slice: x: 4, y: 4 (y_hi: 2, y_lo: 2; y = y_hi * 2 + y_lo), z: 8, core: 2. Of those that a mesh axis runs over, the one named last changes fastest.
Arguments:
- alignment_features: bfloat16 [64, 2048, 256], P(None, ('dp', 'dap')), parts along dimension 1, may hold values from -8 to 8
- layer_norm_gain: float32 [256], replicated, may hold values from 0.1 to 1.9
- layer_norm_bias: float32 [256], replicated, may hold values from -1.2 to 1.2
- left_projection_weight: bfloat16 [256, 32], replicated, may hold values from -0.375 to 0.375
- left_projection_bias: float32 [32], replicated, may hold values from -1.8 to 1.8
- right_projection_weight: bfloat16 [256, 32], replicated, may hold values from -0.375 to 0.375
- right_projection_bias: float32 [32], replicated, may hold values from -1.8 to 1.8
- output_weight: bfloat16 [1024, 128], replicated, may hold values from -0.1875 to 0.1875
- output_bias: float32 [128], replicated, may hold values from -1.8 to 1.8
Outputs:
- pair_update: bfloat16 [2048, 1024, 128], P('dp', 'dap'), parts along dimension 0
The draws below stay inside these ranges and needn't reach their ends.
There are 2 independent parts, one for each index of `dp`. The reference program is written for one: setup_inputs(seed, part) draws one part's arguments, and reference() takes and returns one part's arrays. A program takes and returns all parts, laid end to end along the dimension named above; an argument that names none is the same for every part. Nothing has to cross between parts.
All inputs are finite; a program needn't handle non-finite values.
Results may differ from the reference program's by a relative error of at most 0.0048.
Values may be sent and summed in bfloat16 or wider, within the bound.
No kernel may reach another device: no remote copies, remote signals or barrier semaphores. Data moves between devices by JAX's collectives and lax.ppermute only.
A program may use at most 64 MiB of HBM per device.

```python
import jax
import jax.numpy as jnp
from jax import lax

C_M = 256
HID = 32
C_Z = 128
SEQS = 64
N_RES = 1024


def draw_alignment_features(key, part):
    key = jax.random.fold_in(key, 11)
    key_base, key_noise = jax.random.split(key)
    common = jax.random.normal(key_base, (1, N_RES, C_M), jnp.float32)
    noise = jax.random.normal(key_noise, (SEQS, N_RES, C_M), jnp.float32)
    return jnp.clip(0.1 * common + 0.99 * noise, -8.0, 8.0).astype(jnp.bfloat16)


def scatter_about(rng, dims, deviation, bound, dtype=jnp.bfloat16):
    entries = deviation * jax.random.normal(rng, dims, jnp.float32)
    return jnp.clip(entries, min=-bound, max=bound).astype(dtype)


def setup_inputs(seed: int = 0, part: int = 0) -> dict:
    key_list = jax.random.split(jax.random.key(seed), 10)
    part_splits = jax.random.split(jax.random.fold_in(key_list[9], part), 10)
    return {
        "alignment_features": draw_alignment_features(jax.random.fold_in(jax.random.fold_in(key_list[9], part), 71), part),
        "layer_norm_gain": jnp.clip(1.0 + 0.18 * jax.random.normal(key_list[1], (C_M,), jnp.float32), 0.1, 1.9),
        "layer_norm_bias": scatter_about(key_list[2], (C_M,), 0.2, 1.2, jnp.float32),
        "left_projection_weight": scatter_about(key_list[3], (C_M, HID), C_M ** -0.5, 0.375),
        "left_projection_bias": scatter_about(key_list[4], (HID,), 0.3, 1.8, jnp.float32),
        "right_projection_weight": scatter_about(key_list[5], (C_M, HID), C_M ** -0.5, 0.375),
        "right_projection_bias": scatter_about(key_list[6], (HID,), 0.3, 1.8, jnp.float32),
        "output_weight": scatter_about(key_list[7], (HID * HID, C_Z), (HID * HID) ** -0.5, 0.1875),
        "output_bias": scatter_about(key_list[8], (C_Z,), 0.3, 1.8, jnp.float32),
    }


def apply_layer_norm(feats, gain, offset):
    values = feats.astype(jnp.float32)
    center = lax.optimization_barrier(jnp.mean(values, axis=-1, keepdims=True))
    spread = lax.optimization_barrier(jnp.mean((values - center) ** 2, axis=-1, keepdims=True))
    return ((values - center) * lax.rsqrt(spread + 1e-05) * gain + offset).astype(jnp.bfloat16)

def reference(alignment_features, layer_norm_gain, layer_norm_bias, left_projection_weight, left_projection_bias, right_projection_weight, right_projection_bias, output_weight, output_bias):
    normalized_alignment = apply_layer_norm(alignment_features, layer_norm_gain, layer_norm_bias).astype(jnp.float32)
    left = (jnp.einsum('sic,ch->sih', normalized_alignment, left_projection_weight.astype(jnp.float32)) + left_projection_bias).astype(jnp.bfloat16)
    right = (jnp.einsum('sic,ch->sih', normalized_alignment, right_projection_weight.astype(jnp.float32)) + right_projection_bias).astype(jnp.bfloat16)
    left_rows = jnp.swapaxes(left, 0, 1)
    right_float = jnp.swapaxes(right, 0, 1).astype(jnp.float32)
    scale = 1.0 / SEQS

    def one_row(left_row):
        outer = jnp.einsum('sc,jse->jce', left_row.astype(jnp.float32), right_float) * scale
        outer = outer.astype(jnp.bfloat16).reshape(N_RES, HID * HID)
        return (jnp.dot(outer, output_weight, preferred_element_type=jnp.float32) + output_bias).astype(jnp.bfloat16)
    return lax.map(one_row, left_rows)
```

```python
import jax
import jax.numpy as jnp
from jax import lax
from jax.sharding import PartitionSpec as P

HID = 32
SEQS = 64


def apply_layer_norm(feats, gain, offset):
    values = feats.astype(jnp.float32)
    center = jnp.mean(values, axis=-1, keepdims=True)
    spread = jnp.mean((values - center) ** 2, axis=-1, keepdims=True)
    return ((values - center) * lax.rsqrt(spread + 1e-05) * gain + offset).astype(jnp.bfloat16)


def per_device(
    alignment_features,
    layer_norm_gain,
    layer_norm_bias,
    left_projection_weight,
    left_projection_bias,
    right_projection_weight,
    right_projection_bias,
    output_weight,
    output_bias,
):
    normalized = apply_layer_norm(alignment_features, layer_norm_gain, layer_norm_bias)
    rows = normalized.shape[1]
    left = jnp.einsum(
        "sic,ch->ihs", normalized, left_projection_weight, preferred_element_type=jnp.float32
    )
    left = (left + left_projection_bias[None, :, None]).astype(jnp.bfloat16)
    left = left.reshape(rows, HID * SEQS)
    left_all = lax.all_gather(left, "dap", axis=0, tiled=True)

    right = jnp.einsum(
        "sic,ch->ish", normalized, right_projection_weight, preferred_element_type=jnp.float32
    )
    right = (right + right_projection_bias).astype(jnp.bfloat16)
    weight = output_weight.reshape(HID, HID, -1)
    table = jnp.einsum("jse,cez->csjz", right, weight, preferred_element_type=jnp.float32)
    table = (table * (1.0 / SEQS)).astype(jnp.bfloat16).reshape(HID * SEQS, rows, -1)

    pair = jnp.einsum("ik,kjz->ijz", left_all, table, preferred_element_type=jnp.float32)
    return (pair + output_bias).astype(jnp.bfloat16)


def solution(mesh):
    in_specs = (P(None, ("dp", "dap"), None), P(), P(), P(), P(), P(), P(), P(), P())
    out_specs = P("dp", "dap", None)
    return jax.shard_map(
        per_device, mesh=mesh, in_specs=in_specs, out_specs=out_specs, check_vma=False
    )
```

```python
import functools

import jax
import jax.numpy as jnp
from jax import lax
from jax.experimental import pallas as pl
from jax.experimental.pallas import tpu as pltpu
from jax.sharding import PartitionSpec as P

HID = 32
SEQS = 64
C_Z = 128
NY, NZ, NX, NC = 2, 8, 4, 2
PACK = 4


def device_index(y, z, x, c):
    return ((y % NY * NZ + z % NZ) * NX + x % NX) * NC + c % NC


def shift(move):
    pairs = []
    for y in range(NY):
        for z in range(NZ):
            for x in range(NX):
                for c in range(NC):
                    pairs.append((device_index(y, z, x, c), device_index(*move(y, z, x, c))))
    return pairs


Z_PAIR = shift(lambda y, z, x, c: (y, z ^ 1, x, c))
Z_PLUS = {k: shift(lambda y, z, x, c, k=k: (y, z + k, x, c)) for k in (2, 4, 6)}
Y_PAIR = shift(lambda y, z, x, c: (y + 1, z, x, c))
X_PLUS = {k: shift(lambda y, z, x, c, k=k: (y, z, x + k, c)) for k in (1, 3)}
CORE_PAIR = shift(lambda y, z, x, c: (y, z, x, c + 1))


def send(block, pairs):
    return lax.ppermute(block, "dap", pairs)


def layer_norm(feats, gain, offset):
    values = feats.astype(jnp.float32)
    center = jnp.mean(values, axis=-1, keepdims=True)
    spread = jnp.mean((values - center) ** 2, axis=-1, keepdims=True)
    return (values - center) * lax.rsqrt(spread + 1e-05) * gain + offset


def left_kernel(feats_ref, gain_ref, offset_ref, weight_ref, bias_ref, left_ref):
    groups = SEQS // PACK
    rows = feats_ref.shape[1]
    normed = layer_norm(feats_ref[...], gain_ref[...], offset_ref[...])
    normed = normed.reshape(groups, PACK, rows, -1)
    wide = jnp.concatenate([normed[:, k] for k in range(PACK)], axis=-1)
    wide = wide.reshape(groups * rows, -1).astype(jnp.bfloat16)
    weight = jnp.concatenate([weight_ref[...].astype(jnp.float32)] * PACK, axis=1)
    lane = lax.broadcasted_iota(jnp.int32, weight.shape, 1) // HID
    diagonal = jnp.concatenate(
        [jnp.where(lane == k, weight, 0.0) for k in range(PACK)], axis=0
    ).astype(jnp.bfloat16)
    out = jnp.dot(wide, diagonal, preferred_element_type=jnp.float32) + bias_ref[...]
    for g in range(groups):
        left_ref[:, g * PACK * HID : (g + 1) * PACK * HID] = out[
            g * rows : (g + 1) * rows
        ].astype(jnp.bfloat16)


def table_kernel(feats_ref, gain_ref, offset_ref, weight_ref, bias_ref, out_weight_ref, table_ref, right_ref):
    rows = feats_ref.shape[1]
    normed = layer_norm(feats_ref[...], gain_ref[...], offset_ref[...])
    normed = normed.reshape(SEQS * rows, -1).astype(jnp.bfloat16)
    right = jnp.dot(normed, weight_ref[...], preferred_element_type=jnp.float32) + bias_ref[...]
    right_ref[...] = right.astype(jnp.bfloat16)
    step = 2

    def body(b, carry):
        start = pl.multiple_of(b * step * rows, step * rows)
        part = jnp.dot(
            right_ref[pl.ds(start, step * rows), :],
            out_weight_ref[...],
            preferred_element_type=jnp.float32,
        ) * (1.0 / SEQS)
        part = part.reshape(step * rows, HID, C_Z)
        for s in range(step):
            at = pl.multiple_of((b * step + s) * HID, HID)
            for j in range(rows):
                table_ref[pl.ds(at, HID), j * C_Z : (j + 1) * C_Z] = part[s * rows + j].astype(
                    jnp.bfloat16
                )
        return carry

    lax.fori_loop(0, SEQS // step, body, 0)


def pair_kernel(place_ref, *refs, pieces, aliased):
    lefts = refs[: len(pieces)]
    table_ref, bias_ref = refs[len(pieces) : len(pieces) + 2]
    out_ref, acc_ref = refs[len(pieces) + 2 + aliased :]
    core = place_ref[1]
    for left_ref, (lane, first) in zip(lefts, pieces):
        rows = left_ref.shape[0]
        acc = acc_ref.at[pl.ds(0, rows)]
        acc[...] = jnp.dot(left_ref[...], table_ref[...], preferred_element_type=jnp.float32)
        c = core if lane == 0 else 1 - core

        def body(k, carry, first=first, c=c):
            part = acc_ref[pl.ds(pl.multiple_of(k * 8, 8), 8), :].reshape(8, 8, C_Z) + bias_ref[...]
            out_ref[place_ref[2 + first + k], 0, c] = part.astype(jnp.bfloat16)
            return carry

        lax.fori_loop(0, rows // 8, body, 0, unroll=True)


def pair_block(place, lefts, pieces, table, bias, turn, out):
    aliased = out is not None
    whole = pl.BlockSpec(memory_space=pltpu.VMEM)
    operands = [*lefts, table, bias] + ([out] if aliased else [])
    in_specs = [whole] * (len(lefts) + 2) + ([pl.BlockSpec(memory_space=pl.ANY)] if aliased else [])
    rows = max(left.shape[0] for left in lefts)
    return pl.pallas_call(
        functools.partial(pair_kernel, pieces=pieces, aliased=int(aliased)),
        grid_spec=pltpu.PrefetchScalarGridSpec(
            num_scalar_prefetch=1,
            grid=(1,),
            in_specs=in_specs,
            out_specs=pl.BlockSpec(
                (NY * NZ, 1, NC, 8, 8, C_Z),
                lambda i, place: (0, lax.rem(place[0] + turn, NX), 0, 0, 0, 0),
            ),
            scratch_shapes=[pltpu.VMEM((rows, 8 * C_Z), jnp.float32)],
        ),
        out_shape=jax.ShapeDtypeStruct((NY * NZ, NX, NC, 8, 8, C_Z), jnp.bfloat16),
        input_output_aliases={len(operands): 0} if aliased else {},
        compiler_params=pltpu.CompilerParams(vmem_limit_bytes=24 * 1024 * 1024),
    )(place, *operands)


def per_device(
    alignment_features,
    layer_norm_gain,
    layer_norm_bias,
    left_projection_weight,
    left_projection_bias,
    right_projection_weight,
    right_projection_bias,
    output_weight,
    output_bias,
):
    rows = alignment_features.shape[1]
    gain, offset = layer_norm_gain[None], layer_norm_bias[None]
    vmem = pltpu.CompilerParams(vmem_limit_bytes=32 * 1024 * 1024)
    left = pl.pallas_call(
        left_kernel,
        out_shape=jax.ShapeDtypeStruct((rows, SEQS * HID), jnp.bfloat16),
        compiler_params=vmem,
    )(
        alignment_features,
        gain,
        offset,
        left_projection_weight,
        jnp.tile(left_projection_bias, PACK)[None],
    )
    out_weight = output_weight.reshape(HID, HID, C_Z).transpose(1, 0, 2).reshape(HID, HID * C_Z)
    table = pl.pallas_call(
        table_kernel,
        out_shape=jax.ShapeDtypeStruct((SEQS * HID, rows * C_Z), jnp.bfloat16),
        scratch_shapes=[pltpu.VMEM((SEQS * rows, HID), jnp.bfloat16)],
        compiler_params=vmem,
    )(
        alignment_features,
        gain,
        offset,
        right_projection_weight,
        right_projection_bias[None],
        out_weight,
    )

    me = lax.axis_index("dap")
    core, x, z, y = me % NC, me // NC % NX, me // (NC * NX) % NZ, me // (NC * NX * NZ)
    slots = [
        (y ^ t) * NZ + ((z + NZ - back) % NZ ^ b)
        for t in range(NY)
        for back in (0, 4, 2, 6)
        for b in range(2)
    ]
    place = jnp.stack([x, core] + slots).astype(jnp.int32)
    bias = output_bias[None]

    pair = jnp.concatenate([left, send(left, Z_PAIR)], axis=0)
    ring = jnp.concatenate([pair] + [send(pair, Z_PLUS[k]) for k in (4, 2, 6)], axis=0)
    block = jnp.concatenate([ring, send(ring, Y_PAIR)], axis=0)

    def both(blocks):
        return blocks + [send(b, CORE_PAIR) for b in blocks]

    out = pair_block(place, both([block]), [(0, 0), (1, 0)], table, bias, 0, None)
    low, high = send(block, X_PLUS[1]), send(block, X_PLUS[3])
    half = block.shape[0] // 2
    far = [send(low[:half], X_PLUS[1]), send(high[half:], X_PLUS[3])]
    out = pair_block(place, both([low]), [(0, 0), (1, 0)], table, bias, 3, out)
    out = pair_block(place, both([high]), [(0, 0), (1, 0)], table, bias, 1, out)
    out = pair_block(place, both(far), [(0, 0), (0, 8), (1, 0), (1, 8)], table, bias, 2, out)
    return out.reshape(NY * NZ * NX * NC * 8, 8, C_Z)


def solution(mesh):
    in_specs = (P(None, ("dp", "dap"), None), P(), P(), P(), P(), P(), P(), P(), P())
    out_specs = P("dp", "dap", None)
    return jax.shard_map(
        per_device, mesh=mesh, in_specs=in_specs, out_specs=out_specs, check_vma=False
    )
```

```python
import functools

import jax
import jax.numpy as jnp
from jax import lax
from jax.experimental import pallas as pl
from jax.experimental.pallas import tpu as pltpu
from jax.sharding import PartitionSpec as P

HID = 32
SEQS = 64
C_Z = 128
NY, NZ, NX, NC = 2, 8, 4, 2
PACK = 4


def device_index(y, z, x, c):
    return ((y % NY * NZ + z % NZ) * NX + x % NX) * NC + c % NC


def shift(move):
    pairs = []
    for y in range(NY):
        for z in range(NZ):
            for x in range(NX):
                for c in range(NC):
                    pairs.append((device_index(y, z, x, c), device_index(*move(y, z, x, c))))
    return pairs


Z_PAIR = shift(lambda y, z, x, c: (y, z ^ 1, x, c))
Z_PLUS = {k: shift(lambda y, z, x, c, k=k: (y, z + k, x, c)) for k in (2, 4, 6)}
Y_PAIR = shift(lambda y, z, x, c: (y + 1, z, x, c))
X_PLUS = {k: shift(lambda y, z, x, c, k=k: (y, z, x + k, c)) for k in (1, 3)}
CORE_PAIR = shift(lambda y, z, x, c: (y, z, x, c + 1))


def cost(flops, bytes_accessed):
    return pl.CostEstimate(flops=flops, bytes_accessed=bytes_accessed, transcendentals=0)


def send(block, pairs):
    return lax.ppermute(block, "dap", pairs)


def layer_norm(feats, gain, offset):
    values = feats.astype(jnp.float32)
    center = jnp.mean(values, axis=-1, keepdims=True)
    spread = jnp.mean((values - center) ** 2, axis=-1, keepdims=True)
    return (values - center) * lax.rsqrt(spread + 1e-05) * gain + offset


def dot_last(a, b):
    return lax.dot_general(a, b, (((1,), (1,)), ((), ())), preferred_element_type=jnp.float32)


def left_kernel(feats_ref, gain_ref, offset_ref, weight_ref, bias_ref, left_ref):
    groups = SEQS // PACK
    rows = feats_ref.shape[1]
    normed = layer_norm(feats_ref[...], gain_ref[...], offset_ref[...])
    normed = normed.reshape(groups, PACK, rows, -1)
    wide = jnp.concatenate([normed[:, k] for k in range(PACK)], axis=-1)
    wide = wide.reshape(groups * rows, -1).astype(jnp.bfloat16)
    weight = jnp.concatenate([weight_ref[...].astype(jnp.float32)] * PACK, axis=0)
    turn = lax.broadcasted_iota(jnp.int32, weight.shape, 0) // HID
    diagonal = jnp.concatenate(
        [jnp.where(turn == k, weight, 0.0) for k in range(PACK)], axis=1
    ).astype(jnp.bfloat16)
    bias = jnp.concatenate([bias_ref[...]] * PACK, axis=1)
    out = dot_last(wide, diagonal) + bias
    for g in range(groups):
        left_ref[:, g * PACK * HID : (g + 1) * PACK * HID] = out[
            g * rows : (g + 1) * rows
        ].astype(jnp.bfloat16)


def table_kernel(feats_ref, gain_ref, offset_ref, weight_ref, bias_ref, out_weight_ref, table_ref, right_ref):
    rows = feats_ref.shape[1]
    normed = layer_norm(feats_ref[...], gain_ref[...], offset_ref[...])
    normed = normed.reshape(SEQS * rows, -1).astype(jnp.bfloat16)
    right = dot_last(normed, weight_ref[...]) + bias_ref[...]
    right_ref[...] = right.astype(jnp.bfloat16)
    step = 2

    def body(b, carry):
        start = pl.multiple_of(b * step * rows, step * rows)
        part = jnp.dot(
            right_ref[pl.ds(start, step * rows), :],
            out_weight_ref[...],
            preferred_element_type=jnp.float32,
        ) * (1.0 / SEQS)
        part = part.reshape(step * rows, HID, C_Z)
        for s in range(step):
            at = pl.multiple_of((b * step + s) * HID, HID)
            for j in range(rows):
                table_ref[pl.ds(at, HID), j * C_Z : (j + 1) * C_Z] = part[s * rows + j].astype(
                    jnp.bfloat16
                )
        return carry

    lax.fori_loop(0, SEQS // step, body, 0)


def pair_kernel(place_ref, *refs, pieces, aliased):
    lefts = refs[: len(pieces)]
    table_ref, bias_ref = refs[len(pieces) : len(pieces) + 2]
    out_ref, left_all, acc_ref = refs[len(pieces) + 2 + aliased :]
    core = place_ref[1]
    lanes = out_ref.shape[2]
    rows = lefts[0].shape[0]
    for k, left_ref in enumerate(lefts):
        left_all[k * rows : (k + 1) * rows, :] = left_ref[...]
    acc_ref[...] = jnp.dot(left_all[...], table_ref[...], preferred_element_type=jnp.float32)
    for n, (lane, first) in enumerate(pieces):
        c = core if lane == 0 else 1 - core
        for k in range(rows // 8):
            at = n * rows + k * 8
            part = acc_ref[at : at + 8, :].reshape(8, 8, C_Z) + bias_ref[...]
            out_ref[place_ref[2 + first + k], 0, c if lanes == NC else 0] = part.astype(jnp.bfloat16)


def pair_block(place, lefts, pieces, table, bias, turn, out):
    aliased = out is not None
    whole = pl.BlockSpec(memory_space=pltpu.VMEM)
    operands = [*lefts, table, bias] + ([out] if aliased else [])
    in_specs = [whole] * (len(lefts) + 2) + ([pl.BlockSpec(memory_space=pl.ANY)] if aliased else [])
    rows = sum(left.shape[0] for left in lefts)
    lanes = sorted({lane for lane, _ in pieces})
    if len(lanes) == NC:
        turn_lane = lambda place: 0
    else:
        turn_lane = lambda place: lax.rem(place[1] + lanes[0], NC)
    return pl.pallas_call(
        functools.partial(pair_kernel, pieces=pieces, aliased=int(aliased)),
        grid_spec=pltpu.PrefetchScalarGridSpec(
            num_scalar_prefetch=1,
            grid=(1,),
            in_specs=in_specs,
            out_specs=pl.BlockSpec(
                (NY * NZ, 1, len(lanes), 8, 8, C_Z),
                lambda i, place: (0, lax.rem(place[0] + turn, NX), turn_lane(place), 0, 0, 0),
            ),
            scratch_shapes=[
                pltpu.VMEM((rows, SEQS * HID), jnp.bfloat16),
                pltpu.VMEM((rows, 8 * C_Z), jnp.float32),
            ],
        ),
        out_shape=jax.ShapeDtypeStruct((NY * NZ, NX, NC, 8, 8, C_Z), jnp.bfloat16),
        input_output_aliases={len(operands): 0} if aliased else {},
        compiler_params=pltpu.CompilerParams(vmem_limit_bytes=24 * 1024 * 1024),
        cost_estimate=cost(2 * rows * 2048 * 1024, 10 << 20),
    )(place, *operands)


def per_device(
    alignment_features,
    layer_norm_gain,
    layer_norm_bias,
    left_projection_weight,
    left_projection_bias,
    right_projection_weight,
    right_projection_bias,
    output_weight,
    output_bias,
):
    rows = alignment_features.shape[1]
    gain, offset = layer_norm_gain[None], layer_norm_bias[None]
    vmem = pltpu.CompilerParams(vmem_limit_bytes=32 * 1024 * 1024)
    left = pl.pallas_call(
        left_kernel,
        out_shape=jax.ShapeDtypeStruct((rows, SEQS * HID), jnp.bfloat16),
        compiler_params=pltpu.CompilerParams(vmem_limit_bytes=60 * 1024 * 1024),
    )(
        alignment_features,
        gain,
        offset,
        left_projection_weight.T,
        left_projection_bias[None],
    )
    out_weight = output_weight.reshape(HID, HID, C_Z).transpose(1, 0, 2).reshape(HID, HID * C_Z)
    table = pl.pallas_call(
        table_kernel,
        out_shape=jax.ShapeDtypeStruct((SEQS * HID, rows * C_Z), jnp.bfloat16),
        scratch_shapes=[pltpu.VMEM((SEQS * rows, HID), jnp.bfloat16)],
        compiler_params=vmem,
        cost_estimate=cost(1 << 30, 24 << 20),
    )(
        alignment_features,
        gain,
        offset,
        right_projection_weight.T,
        right_projection_bias[None],
        out_weight,
    )

    me = lax.axis_index("dap")
    core, x, z, y = me % NC, me // NC % NX, me // (NC * NX) % NZ, me // (NC * NX * NZ)
    slots = [
        (y ^ t) * NZ + ((z + NZ - back) % NZ ^ b)
        for t in range(NY)
        for back in (0, 4, 2, 6)
        for b in range(2)
    ]
    place = jnp.stack([x, core] + slots).astype(jnp.int32)
    bias = output_bias[None]

    pair = jnp.concatenate([left, send(left, Z_PAIR)], axis=0)
    ring = jnp.concatenate([pair] + [send(pair, Z_PLUS[k]) for k in (4, 2, 6)], axis=0)
    block = jnp.concatenate([ring, send(ring, Y_PAIR)], axis=0)

    def other(blocks):
        return [send(b, CORE_PAIR) for b in blocks]

    whole = [(0, 0), (1, 0)]
    low, high = send(block, X_PLUS[1]), send(block, X_PLUS[3])
    out = pair_block(place, [block] + other([block]), whole, table, bias, 0, None)
    low, high, table, out = lax.optimization_barrier((low, high, table, out))
    half = block.shape[0] // 2
    far = [send(low[:half], X_PLUS[1]), send(high[half:], X_PLUS[3])]
    out = pair_block(place, [low] + other([low]), whole, table, bias, 3, out)
    out = pair_block(place, [high] + other([high]), whole, table, bias, 1, out)
    far[0], far[1], out = lax.optimization_barrier((far[0], far[1], out))
    far_other = other(far)
    out = pair_block(place, far, [(0, 0), (0, 8)], table, bias, 2, out)
    out = pair_block(place, far_other, [(1, 0), (1, 8)], table, bias, 2, out)
    return out.reshape(NY * NZ * NX * NC * 8, 8, C_Z)


def solution(mesh):
    in_specs = (P(None, ("dp", "dap"), None), P(), P(), P(), P(), P(), P(), P(), P())
    out_specs = P("dp", "dap", None)
    return jax.shard_map(
        per_device, mesh=mesh, in_specs=in_specs, out_specs=out_specs, check_vma=False
    )
```

```python
import functools

import jax
import jax.numpy as jnp
from jax import lax
from jax.experimental import pallas as pl
from jax.experimental.pallas import tpu as pltpu
from jax.sharding import PartitionSpec as P

HID = 32
SEQS = 64
C_Z = 128
NY, NZ, NX, NC = 2, 8, 4, 2
PACK = 4


def device_index(y, z, x, c):
    return ((y % NY * NZ + z % NZ) * NX + x % NX) * NC + c % NC


def shift(move):
    pairs = []
    for y in range(NY):
        for z in range(NZ):
            for x in range(NX):
                for c in range(NC):
                    pairs.append((device_index(y, z, x, c), device_index(*move(y, z, x, c))))
    return pairs


def side(c):
    return 1 - 2 * c


Z_EVEN = {k: shift(lambda y, z, x, c, k=k: (y, z + k, x, c)) for k in (2, 4, 6)}
Y_PAIR = shift(lambda y, z, x, c: (y + 1, z, x, c))
Z_PAIR = shift(lambda y, z, x, c: (y, z ^ 1, x, c))
YZ_PAIR = shift(lambda y, z, x, c: (y + 1, z ^ 1, x, c))
X_SIDE = shift(lambda y, z, x, c: (y, z, x + side(c), c))
X_BACK = shift(lambda y, z, x, c: (y, z, x - side(c), c))
CORE_PAIR = shift(lambda y, z, x, c: (y, z, x, c + 1))
PARTS = [(t, b, back) for b in range(2) for t in range(NY) for back in (0, 4, 2, 6)]


def cost(flops, bytes_accessed):
    return pl.CostEstimate(flops=flops, bytes_accessed=bytes_accessed, transcendentals=0)


def send(block, pairs):
    return lax.ppermute(block, "dap", pairs)


def layer_norm(feats, gain, offset):
    values = feats.astype(jnp.float32)
    center = jnp.mean(values, axis=-1, keepdims=True)
    spread = jnp.mean((values - center) ** 2, axis=-1, keepdims=True)
    return (values - center) * lax.rsqrt(spread + 1e-05) * gain + offset


def dot_last(a, b):
    return lax.dot_general(a, b, (((1,), (1,)), ((), ())), preferred_element_type=jnp.float32)


def left_kernel(feats_ref, gain_ref, offset_ref, weight_ref, bias_ref, left_ref):
    groups = SEQS // PACK
    rows = feats_ref.shape[1]
    normed = layer_norm(feats_ref[...], gain_ref[...], offset_ref[...])
    normed = normed.reshape(groups, PACK, rows, -1)
    wide = jnp.concatenate([normed[:, k] for k in range(PACK)], axis=-1)
    wide = wide.reshape(groups * rows, -1).astype(jnp.bfloat16)
    weight = jnp.concatenate([weight_ref[...].astype(jnp.float32)] * PACK, axis=0)
    turn = lax.broadcasted_iota(jnp.int32, weight.shape, 0) // HID
    diagonal = jnp.concatenate(
        [jnp.where(turn == k, weight, 0.0) for k in range(PACK)], axis=1
    ).astype(jnp.bfloat16)
    bias = jnp.concatenate([bias_ref[...]] * PACK, axis=1)
    out = dot_last(wide, diagonal) + bias
    for g in range(groups):
        left_ref[:, g * PACK * HID : (g + 1) * PACK * HID] = out[
            g * rows : (g + 1) * rows
        ].astype(jnp.bfloat16)


def table_kernel(feats_ref, gain_ref, offset_ref, weight_ref, bias_ref, out_weight_ref, table_ref, right_ref):
    rows = feats_ref.shape[1]
    normed = layer_norm(feats_ref[...], gain_ref[...], offset_ref[...])
    normed = normed.reshape(SEQS * rows, -1).astype(jnp.bfloat16)
    right = dot_last(normed, weight_ref[...]) + bias_ref[...]
    right_ref[...] = right.astype(jnp.bfloat16)
    step = 2

    def body(b, carry):
        start = pl.multiple_of(b * step * rows, step * rows)
        part = jnp.dot(
            right_ref[pl.ds(start, step * rows), :],
            out_weight_ref[...],
            preferred_element_type=jnp.float32,
        ) * (1.0 / SEQS)
        part = part.reshape(step * rows, HID, C_Z)
        for s in range(step):
            at = pl.multiple_of((b * step + s) * HID, HID)
            for j in range(rows):
                table_ref[pl.ds(at, HID), j * C_Z : (j + 1) * C_Z] = part[s * rows + j].astype(
                    jnp.bfloat16
                )
        return carry

    lax.fori_loop(0, SEQS // step, body, 0)


def pair_kernel(*refs, pieces, aliased):
    lefts = refs[: len(pieces)]
    table_ref, bias_ref = refs[len(pieces) : len(pieces) + 2]
    out_ref, left_all, acc_ref, ready, sems = refs[len(pieces) + 2 + aliased :]
    rows = lefts[0].shape[0]
    for n, left_ref in enumerate(lefts):
        left_all[n * rows : (n + 1) * rows, :] = left_ref[...]
    acc_ref[...] = jnp.dot(left_all[...], table_ref[...], preferred_element_type=jnp.float32)
    me = lax.axis_index("dap")
    core = lax.rem(me, NC)
    x = lax.rem(lax.div(me, NC), NX)
    z = lax.rem(lax.div(me, NC * NX), NZ)
    y = lax.div(me, NC * NX * NZ)
    copies = []
    for n, (lane, ahead) in enumerate(pieces):
        c = core if lane == 0 else 1 - core
        to_x = lax.rem(x + ahead * side(core) + NX, NX)
        for k, (t, b, back) in enumerate(PARTS):
            slot = n * len(PARTS) + k
            part = acc_ref[slot * 8 : slot * 8 + 8, :].reshape(8, 8, C_Z) + bias_ref[...]
            ready[slot] = part.astype(jnp.bfloat16)
            to_y = lax.rem(y + t, NY)
            to_z = lax.rem((z + b * (1 - 2 * lax.rem(z, 2))) - back + NZ, NZ)
            to = ((to_y * NZ + to_z) * NX + to_x) * NC + c
            copy = pltpu.make_async_copy(ready.at[slot], out_ref.at[to], sems.at[slot])
            copy.start()
            copies.append(copy)
    for copy in copies:
        copy.wait()


def pair_block(lefts, pieces, table, bias, out):
    aliased = out is not None
    vmem, anywhere = pl.BlockSpec(memory_space=pltpu.VMEM), pl.BlockSpec(memory_space=pl.ANY)
    operands = [*lefts, table, bias] + ([out] if aliased else [])
    rows = sum(left.shape[0] for left in lefts)
    depth, width = table.shape
    blocks = rows // 8
    return pl.pallas_call(
        functools.partial(pair_kernel, pieces=pieces, aliased=int(aliased)),
        in_specs=[vmem] * (len(lefts) + 2) + ([anywhere] if aliased else []),
        out_specs=anywhere,
        out_shape=jax.ShapeDtypeStruct((NY * NZ * NX * NC, 8, 8, C_Z), jnp.bfloat16),
        scratch_shapes=[
            pltpu.VMEM((rows, depth), jnp.bfloat16),
            pltpu.VMEM((rows, width), jnp.float32),
            pltpu.VMEM((blocks, 8, 8, C_Z), jnp.bfloat16),
            pltpu.SemaphoreType.DMA((blocks,)),
        ],
        input_output_aliases={len(operands) - 1: 0} if aliased else {},
        compiler_params=pltpu.CompilerParams(vmem_limit_bytes=24 * 1024 * 1024),
        cost_estimate=cost(2 * rows * depth * width, 10 << 20),
    )(*operands)


def per_device(
    alignment_features,
    layer_norm_gain,
    layer_norm_bias,
    left_projection_weight,
    left_projection_bias,
    right_projection_weight,
    right_projection_bias,
    output_weight,
    output_bias,
):
    rows = alignment_features.shape[1]
    gain, offset = layer_norm_gain[None], layer_norm_bias[None]
    vmem = pltpu.CompilerParams(vmem_limit_bytes=32 * 1024 * 1024)
    left = pl.pallas_call(
        left_kernel,
        out_shape=jax.ShapeDtypeStruct((rows, SEQS * HID), jnp.bfloat16),
        compiler_params=pltpu.CompilerParams(vmem_limit_bytes=60 * 1024 * 1024),
    )(
        alignment_features,
        gain,
        offset,
        left_projection_weight.T,
        left_projection_bias[None],
    )
    out_weight = output_weight.reshape(HID, HID, C_Z).transpose(1, 0, 2).reshape(HID, HID * C_Z)
    table = pl.pallas_call(
        table_kernel,
        out_shape=jax.ShapeDtypeStruct((SEQS * HID, rows * C_Z), jnp.bfloat16),
        scratch_shapes=[pltpu.VMEM((SEQS * rows, HID), jnp.bfloat16)],
        compiler_params=vmem,
        cost_estimate=cost(1 << 30, 24 << 20),
    )(
        alignment_features,
        gain,
        offset,
        right_projection_weight.T,
        right_projection_bias[None],
        out_weight,
    )

    bias = output_bias[None]

    ring = jnp.concatenate([left] + [send(left, Z_EVEN[k]) for k in (4, 2, 6)], axis=0)
    block = jnp.concatenate(
        [ring, send(ring, Y_PAIR), send(ring, Z_PAIR), send(ring, YZ_PAIR)], axis=0
    )
    ahead, behind = send(block, X_BACK), send(block, X_SIDE)
    out = pair_block([block, send(block, CORE_PAIR)], [(0, 0), (1, 0)], table, bias, None)
    ahead, behind, table, out = lax.optimization_barrier((ahead, behind, table, out))
    others = [send(ahead, CORE_PAIR), send(behind, CORE_PAIR)]
    far = send(behind, X_SIDE)
    out = pair_block([ahead, behind], [(0, 1), (0, -1)], table, bias, out)
    out = pair_block(others, [(1, -1), (1, 1)], table, bias, out)
    far, out = lax.optimization_barrier((far, out))
    far_other = send(far, CORE_PAIR)
    out = pair_block([far], [(0, 2)], table, bias, out)
    out = pair_block([far_other], [(1, 2)], table, bias, out)
    return out.reshape(NY * NZ * NX * NC * 8, 8, C_Z)


def solution(mesh):
    in_specs = (P(None, ("dp", "dap"), None), P(), P(), P(), P(), P(), P(), P(), P())
    out_specs = P("dp", "dap", None)
    return jax.shard_map(
        per_device, mesh=mesh, in_specs=in_specs, out_specs=out_specs, check_vma=False
    )
```

```python
import functools

import jax
import jax.numpy as jnp
from jax import lax
from jax.experimental import pallas as pl
from jax.experimental.pallas import tpu as pltpu
from jax.sharding import PartitionSpec as P

HID = 32
SEQS = 64
C_Z = 128
NY, NZ, NX, NC = 2, 8, 4, 2
PACK = 4


def device_index(y, z, x, c):
    return ((y % NY * NZ + z % NZ) * NX + x % NX) * NC + c % NC


def shift(move):
    pairs = []
    for y in range(NY):
        for z in range(NZ):
            for x in range(NX):
                for c in range(NC):
                    pairs.append((device_index(y, z, x, c), device_index(*move(y, z, x, c))))
    return pairs


def side(c):
    return 1 - 2 * c


Z_EVEN = {k: shift(lambda y, z, x, c, k=k: (y, z + k, x, c)) for k in (2, 4, 6)}
Y_PAIR = shift(lambda y, z, x, c: (y + 1, z, x, c))
Z_PAIR = shift(lambda y, z, x, c: (y, z ^ 1, x, c))
YZ_PAIR = shift(lambda y, z, x, c: (y + 1, z ^ 1, x, c))
X_SIDE = shift(lambda y, z, x, c: (y, z, x + side(c), c))
X_BACK = shift(lambda y, z, x, c: (y, z, x - side(c), c))
CORE_PAIR = shift(lambda y, z, x, c: (y, z, x, c + 1))
BACKS = (4, 2, 6)
PARTS = [(t, b, back) for b in range(2) for t in range(NY) for back in (0, *BACKS)]


def cost(flops, bytes_accessed):
    return pl.CostEstimate(flops=flops, bytes_accessed=bytes_accessed, transcendentals=0)


def send(block, pairs):
    return lax.ppermute(block, "dap", pairs)


def join(blocks):
    rows = blocks[0].shape[0]
    whole = jnp.zeros((rows * len(blocks), blocks[0].shape[1]), blocks[0].dtype)
    for k, block in enumerate(blocks):
        whole = lax.dynamic_update_slice(whole, block, (k * rows, 0))
    return whole


def layer_norm(feats, gain, offset):
    values = feats.astype(jnp.float32)
    center = jnp.mean(values, axis=-1, keepdims=True)
    spread = jnp.mean((values - center) ** 2, axis=-1, keepdims=True)
    return (values - center) * lax.rsqrt(spread + 1e-05) * gain + offset


def dot_last(a, b):
    return lax.dot_general(a, b, (((1,), (1,)), ((), ())), preferred_element_type=jnp.float32)


def left_kernel(feats_ref, gain_ref, offset_ref, weight_ref, bias_ref, left_ref):
    groups = SEQS // PACK
    rows = feats_ref.shape[1]
    normed = layer_norm(feats_ref[...], gain_ref[...], offset_ref[...])
    normed = normed.reshape(groups, PACK, rows, -1)
    wide = jnp.concatenate([normed[:, k] for k in range(PACK)], axis=-1)
    wide = wide.reshape(groups * rows, -1).astype(jnp.bfloat16)
    weight = jnp.concatenate([weight_ref[...].astype(jnp.float32)] * PACK, axis=0)
    turn = lax.broadcasted_iota(jnp.int32, weight.shape, 0) // HID
    diagonal = jnp.concatenate(
        [jnp.where(turn == k, weight, 0.0) for k in range(PACK)], axis=1
    ).astype(jnp.bfloat16)
    bias = jnp.concatenate([bias_ref[...]] * PACK, axis=1)
    out = dot_last(wide, diagonal) + bias
    for g in range(groups):
        left_ref[:, g * PACK * HID : (g + 1) * PACK * HID] = out[
            g * rows : (g + 1) * rows
        ].astype(jnp.bfloat16)


def table_kernel(feats_ref, gain_ref, offset_ref, weight_ref, bias_ref, out_weight_ref, table_ref, right_ref):
    rows = feats_ref.shape[1]
    normed = layer_norm(feats_ref[...], gain_ref[...], offset_ref[...])
    normed = normed.reshape(SEQS * rows, -1).astype(jnp.bfloat16)
    right = dot_last(normed, weight_ref[...]) + bias_ref[...]
    right_ref[...] = right.astype(jnp.bfloat16)
    step = 16

    def body(b, carry):
        start = pl.multiple_of(b * step * rows, step * rows)
        part = jnp.dot(
            right_ref[pl.ds(start, step * rows), :],
            out_weight_ref[...],
            preferred_element_type=jnp.float32,
        ) * (1.0 / SEQS)
        part = part.reshape(step * rows, HID, C_Z)
        for s in range(step):
            at = pl.multiple_of((b * step + s) * HID, HID)
            for j in range(rows):
                table_ref[pl.ds(at, HID), j * C_Z : (j + 1) * C_Z] = part[s * rows + j].astype(
                    jnp.bfloat16
                )
        return carry

    lax.fori_loop(0, SEQS // step, body, 0)


def pair_kernel(*refs, pieces, aliased):
    lefts = refs[: len(pieces)]
    table_ref, bias_ref = refs[len(pieces) : len(pieces) + 2]
    out_ref, left_all, acc_ref, ready, sems = refs[len(pieces) + 2 + aliased :]
    rows = lefts[0].shape[0]
    if len(lefts) == 1:
        left_all = lefts[0]
    else:
        for n, left_ref in enumerate(lefts):
            left_all[n * rows : (n + 1) * rows, :] = left_ref[...]
    acc_ref[...] = jnp.dot(left_all[...], table_ref[...], preferred_element_type=jnp.float32)
    me = lax.axis_index("dap")
    core = lax.rem(me, NC)
    x = lax.rem(lax.div(me, NC), NX)
    z = lax.rem(lax.div(me, NC * NX), NZ)
    y = lax.div(me, NC * NX * NZ)
    copies = []
    for n, (lane, ahead) in enumerate(pieces):
        c = core if lane == 0 else 1 - core
        to_x = lax.rem(x + ahead * side(core) + NX, NX)
        for k, (t, b, back) in enumerate(PARTS):
            slot = n * len(PARTS) + k
            part = acc_ref[slot * 8 : slot * 8 + 8, :].reshape(8, 8, C_Z) + bias_ref[...]
            ready[slot] = part.astype(jnp.bfloat16)
            to_y = lax.rem(y + t, NY)
            to_z = lax.rem((z + b * (1 - 2 * lax.rem(z, 2))) - back + NZ, NZ)
            to = ((to_y * NZ + to_z) * NX + to_x) * NC + c
            copy = pltpu.make_async_copy(ready.at[slot], out_ref.at[to], sems.at[slot])
            copy.start()
            copies.append(copy)
    for copy in copies:
        copy.wait()


def pair_block(lefts, pieces, table, bias, out):
    aliased = out is not None
    vmem, anywhere = pl.BlockSpec(memory_space=pltpu.VMEM), pl.BlockSpec(memory_space=pl.ANY)
    operands = [*lefts, table, bias] + ([out] if aliased else [])
    rows = sum(left.shape[0] for left in lefts)
    depth, width = table.shape
    blocks = rows // 8
    return pl.pallas_call(
        functools.partial(pair_kernel, pieces=pieces, aliased=int(aliased)),
        in_specs=[vmem] * (len(lefts) + 2) + ([anywhere] if aliased else []),
        out_specs=anywhere,
        out_shape=jax.ShapeDtypeStruct((NY * NZ * NX * NC, 8, 8, C_Z), jnp.bfloat16),
        scratch_shapes=[
            pltpu.VMEM((rows, depth), jnp.bfloat16),
            pltpu.VMEM((rows, width), jnp.float32),
            pltpu.VMEM((blocks, 8, 8, C_Z), jnp.bfloat16),
            pltpu.SemaphoreType.DMA((blocks,)),
        ],
        input_output_aliases={len(operands) - 1: 0} if aliased else {},
        compiler_params=pltpu.CompilerParams(vmem_limit_bytes=24 * 1024 * 1024),
        cost_estimate=cost(2 * rows * depth * width, 10 << 20),
    )(*operands)


def per_device(
    alignment_features,
    layer_norm_gain,
    layer_norm_bias,
    left_projection_weight,
    left_projection_bias,
    right_projection_weight,
    right_projection_bias,
    output_weight,
    output_bias,
):
    rows = alignment_features.shape[1]
    gain, offset = layer_norm_gain[None], layer_norm_bias[None]
    vmem = pltpu.CompilerParams(vmem_limit_bytes=32 * 1024 * 1024)
    left = pl.pallas_call(
        left_kernel,
        out_shape=jax.ShapeDtypeStruct((rows, SEQS * HID), jnp.bfloat16),
        compiler_params=pltpu.CompilerParams(vmem_limit_bytes=60 * 1024 * 1024),
    )(
        alignment_features,
        gain,
        offset,
        left_projection_weight.T,
        left_projection_bias[None],
    )
    out_weight = output_weight.reshape(HID, HID, C_Z).transpose(1, 0, 2).reshape(HID, HID * C_Z)
    table = pl.pallas_call(
        table_kernel,
        out_shape=jax.ShapeDtypeStruct((SEQS * HID, rows * C_Z), jnp.bfloat16),
        scratch_shapes=[pltpu.VMEM((SEQS * rows, HID), jnp.bfloat16)],
        compiler_params=vmem,
        cost_estimate=cost(1 << 30, 24 << 20),
    )(
        alignment_features,
        gain,
        offset,
        right_projection_weight.T,
        right_projection_bias[None],
        out_weight,
    )

    bias = output_bias[None]

    ring = join([left] + [send(left, Z_EVEN[k]) for k in BACKS])
    block = join([ring, send(ring, Y_PAIR), send(ring, Z_PAIR), send(ring, YZ_PAIR)])
    ahead, behind = send(block, X_BACK), send(block, X_SIDE)
    out = pair_block([block, send(block, CORE_PAIR)], [(0, 0), (1, 0)], table, bias, None)
    ahead, behind, table, out = lax.optimization_barrier((ahead, behind, table, out))
    others = [send(ahead, CORE_PAIR), send(behind, CORE_PAIR)]
    far = send(behind, X_SIDE)
    out = pair_block([ahead, behind], [(0, 1), (0, -1)], table, bias, out)
    out = pair_block(others, [(1, -1), (1, 1)], table, bias, out)
    far, out = lax.optimization_barrier((far, out))
    far_other = send(far, CORE_PAIR)
    out = pair_block([far], [(0, 2)], table, bias, out)
    out = pair_block([far_other], [(1, 2)], table, bias, out)
    return out.reshape(NY * NZ * NX * NC * 8, 8, C_Z)


def solution(mesh):
    in_specs = (P(None, ("dp", "dap"), None), P(), P(), P(), P(), P(), P(), P(), P())
    out_specs = P("dp", "dap", None)
    return jax.shard_map(
        per_device, mesh=mesh, in_specs=in_specs, out_specs=out_specs, check_vma=False
    )
```

```python
import functools

import jax
import jax.numpy as jnp
from jax import lax
from jax.experimental import pallas as pl
from jax.experimental.pallas import tpu as pltpu
from jax.sharding import PartitionSpec as P

HID = 32
SEQS = 64
C_Z = 128
NY, NZ, NX, NC = 2, 8, 4, 2
PACK = 4


def device_index(y, z, x, c):
    return ((y % NY * NZ + z % NZ) * NX + x % NX) * NC + c % NC


def shift(move):
    pairs = []
    for y in range(NY):
        for z in range(NZ):
            for x in range(NX):
                for c in range(NC):
                    pairs.append((device_index(y, z, x, c), device_index(*move(y, z, x, c))))
    return pairs


def side(c):
    return 1 - 2 * c


Z_EVEN = {k: shift(lambda y, z, x, c, k=k: (y, z + k, x, c)) for k in (2, 4, 6)}
Y_PAIR = shift(lambda y, z, x, c: (y + 1, z, x, c))
Z_PAIR = shift(lambda y, z, x, c: (y, z ^ 1, x, c))
YZ_PAIR = shift(lambda y, z, x, c: (y + 1, z ^ 1, x, c))
X_SIDE = shift(lambda y, z, x, c: (y, z, x + side(c), c))
X_BACK = shift(lambda y, z, x, c: (y, z, x - side(c), c))
CORE_PAIR = shift(lambda y, z, x, c: (y, z, x, c + 1))
BACKS = (4, 2, 6)
PARTS = [(t, b, back) for b in range(2) for t in range(NY) for back in (0, *BACKS)]


def cost(flops, bytes_accessed):
    return pl.CostEstimate(flops=flops, bytes_accessed=bytes_accessed, transcendentals=0)


def send(block, pairs):
    return lax.ppermute(block, "dap", pairs)


def join(blocks):
    rows = blocks[0].shape[0]
    whole = jnp.zeros((rows * len(blocks), blocks[0].shape[1]), blocks[0].dtype)
    for k, block in enumerate(blocks):
        whole = lax.dynamic_update_slice(whole, block, (k * rows, 0))
    return whole


def layer_norm(feats, gain, offset):
    values = feats.astype(jnp.float32)
    center = jnp.mean(values, axis=-1, keepdims=True)
    spread = jnp.mean((values - center) ** 2, axis=-1, keepdims=True)
    return (values - center) * lax.rsqrt(spread + 1e-05) * gain + offset


def dot_last(a, b):
    return lax.dot_general(a, b, (((1,), (1,)), ((), ())), preferred_element_type=jnp.float32)


def left_kernel(feats_ref, gain_ref, offset_ref, weight_ref, bias_ref, left_ref):
    groups = SEQS // PACK
    rows = feats_ref.shape[1]
    normed = layer_norm(feats_ref[...], gain_ref[...], offset_ref[...])
    normed = normed.reshape(groups, PACK, rows, -1)
    wide = jnp.concatenate([normed[:, k] for k in range(PACK)], axis=-1)
    wide = wide.reshape(groups * rows, -1).astype(jnp.bfloat16)
    weight = jnp.concatenate([weight_ref[...].astype(jnp.float32)] * PACK, axis=0)
    turn = lax.broadcasted_iota(jnp.int32, weight.shape, 0) // HID
    diagonal = jnp.concatenate(
        [jnp.where(turn == k, weight, 0.0) for k in range(PACK)], axis=1
    ).astype(jnp.bfloat16)
    bias = jnp.concatenate([bias_ref[...]] * PACK, axis=1)
    out = dot_last(wide, diagonal) + bias
    for g in range(groups):
        left_ref[:, g * PACK * HID : (g + 1) * PACK * HID] = out[
            g * rows : (g + 1) * rows
        ].astype(jnp.bfloat16)


def table_kernel(feats_ref, gain_ref, offset_ref, weight_ref, bias_ref, out_weight_ref, table_ref, right_ref):
    rows = feats_ref.shape[1]
    normed = layer_norm(feats_ref[...], gain_ref[...], offset_ref[...])
    normed = normed.reshape(SEQS * rows, -1).astype(jnp.bfloat16)
    right = dot_last(normed, weight_ref[...]) + bias_ref[...]
    right_ref[...] = right.astype(jnp.bfloat16)
    step = 16

    def body(b, carry):
        start = pl.multiple_of(b * step * rows, step * rows)
        part = jnp.dot(
            right_ref[pl.ds(start, step * rows), :],
            out_weight_ref[...],
            preferred_element_type=jnp.float32,
        ) * (1.0 / SEQS)
        part = part.reshape(step * rows, HID, C_Z)
        for s in range(step):
            at = pl.multiple_of((b * step + s) * HID, HID)
            for j in range(rows):
                table_ref[pl.ds(at, HID), j * C_Z : (j + 1) * C_Z] = part[s * rows + j].astype(
                    jnp.bfloat16
                )
        return carry

    lax.fori_loop(0, SEQS // step, body, 0)


def pair_kernel(*refs, pieces, aliased):
    lefts = refs[: len(pieces)]
    table_ref, bias_ref = refs[len(pieces) : len(pieces) + 2]
    out_ref, left_all, acc_ref, ready, sems = refs[len(pieces) + 2 + aliased :]
    rows = lefts[0].shape[0]
    if len(lefts) == 1:
        left_all = lefts[0]
    else:
        for n, left_ref in enumerate(lefts):
            left_all[n * rows : (n + 1) * rows, :] = left_ref[...]
    acc_ref[...] = jnp.dot(left_all[...], table_ref[...], preferred_element_type=jnp.float32)
    me = lax.axis_index("dap")
    core = lax.rem(me, NC)
    x = lax.rem(lax.div(me, NC), NX)
    z = lax.rem(lax.div(me, NC * NX), NZ)
    y = lax.div(me, NC * NX * NZ)
    copies = []
    for n, (lane, ahead) in enumerate(pieces):
        c = core if lane == 0 else 1 - core
        to_x = lax.rem(x + ahead * side(core) + NX, NX)
        count = rows // 8
        first = n * count % len(PARTS)
        for k, (t, b, back) in enumerate(PARTS[first : first + count]):
            slot = n * count + k
            part = acc_ref[slot * 8 : slot * 8 + 8, :].reshape(8, 8, C_Z) + bias_ref[...]
            ready[slot] = part.astype(jnp.bfloat16)
            to_y = lax.rem(y + t, NY)
            to_z = lax.rem((z + b * (1 - 2 * lax.rem(z, 2))) - back + NZ, NZ)
            to = ((to_y * NZ + to_z) * NX + to_x) * NC + c
            copy = pltpu.make_async_copy(ready.at[slot], out_ref.at[to], sems.at[slot])
            copy.start()
            copies.append(copy)
    for copy in copies:
        copy.wait()


def pair_block(lefts, pieces, table, bias, out, reach=10 << 20):
    aliased = out is not None
    vmem, anywhere = pl.BlockSpec(memory_space=pltpu.VMEM), pl.BlockSpec(memory_space=pl.ANY)
    operands = [*lefts, table, bias] + ([out] if aliased else [])
    rows = sum(left.shape[0] for left in lefts)
    depth, width = table.shape
    blocks = rows // 8
    return pl.pallas_call(
        functools.partial(pair_kernel, pieces=pieces, aliased=int(aliased)),
        in_specs=[vmem] * (len(lefts) + 2) + ([anywhere] if aliased else []),
        out_specs=anywhere,
        out_shape=jax.ShapeDtypeStruct((NY * NZ * NX * NC, 8, 8, C_Z), jnp.bfloat16),
        scratch_shapes=[
            pltpu.VMEM((rows, depth), jnp.bfloat16),
            pltpu.VMEM((rows, width), jnp.float32),
            pltpu.VMEM((blocks, 8, 8, C_Z), jnp.bfloat16),
            pltpu.SemaphoreType.DMA((blocks,)),
        ],
        input_output_aliases={len(operands) - 1: 0} if aliased else {},
        compiler_params=pltpu.CompilerParams(vmem_limit_bytes=24 * 1024 * 1024),
        cost_estimate=cost(2 * rows * depth * width, reach),
    )(*operands)


def per_device(
    alignment_features,
    layer_norm_gain,
    layer_norm_bias,
    left_projection_weight,
    left_projection_bias,
    right_projection_weight,
    right_projection_bias,
    output_weight,
    output_bias,
):
    rows = alignment_features.shape[1]
    gain, offset = layer_norm_gain[None], layer_norm_bias[None]
    vmem = pltpu.CompilerParams(vmem_limit_bytes=32 * 1024 * 1024)
    left = pl.pallas_call(
        left_kernel,
        out_shape=pltpu.VMEM((rows, SEQS * HID), jnp.bfloat16),
        out_specs=pl.BlockSpec(memory_space=pltpu.VMEM),
        compiler_params=pltpu.CompilerParams(vmem_limit_bytes=60 * 1024 * 1024),
    )(
        alignment_features,
        gain,
        offset,
        left_projection_weight.T,
        left_projection_bias[None],
    )
    out_weight = output_weight.reshape(HID, HID, C_Z).transpose(1, 0, 2).reshape(HID, HID * C_Z)
    table = pl.pallas_call(
        table_kernel,
        out_shape=jax.ShapeDtypeStruct((SEQS * HID, rows * C_Z), jnp.bfloat16),
        scratch_shapes=[pltpu.VMEM((SEQS * rows, HID), jnp.bfloat16)],
        compiler_params=vmem,
        cost_estimate=cost(1 << 30, 24 << 20),
    )(
        alignment_features,
        gain,
        offset,
        right_projection_weight.T,
        right_projection_bias[None],
        out_weight,
    )

    bias = output_bias[None]

    ring = join([left] + [send(left, Z_EVEN[k]) for k in BACKS])
    block = join([ring, send(ring, Y_PAIR), send(ring, Z_PAIR), send(ring, YZ_PAIR)])
    ahead, behind = send(block, X_BACK), send(block, X_SIDE)
    out = pair_block([block, send(block, CORE_PAIR)], [(0, 0), (1, 0)], table, bias, None)
    ahead, behind, table, out = lax.optimization_barrier((ahead, behind, table, out))
    far = send(behind, X_SIDE)
    out = pair_block([ahead, behind], [(0, 1), (0, -1)], table, bias, out, 100 << 20)
    ahead, behind, out = lax.optimization_barrier((ahead, behind, out))
    half = block.shape[0] // 2
    others = [send(part, CORE_PAIR) for b in (ahead, behind) for part in (b[:half], b[half:])]
    out = pair_block(others, [(1, -1), (1, -1), (1, 1), (1, 1)], table, bias, out, 1 << 10)
    far, out = lax.optimization_barrier((far, out))
    far_other = send(far, CORE_PAIR)
    out = pair_block([far], [(0, 2)], table, bias, out)
    out = pair_block([far_other], [(1, 2)], table, bias, out)
    return out.reshape(NY * NZ * NX * NC * 8, 8, C_Z)


def solution(mesh):
    in_specs = (P(None, ("dp", "dap"), None), P(), P(), P(), P(), P(), P(), P(), P())
    out_specs = P("dp", "dap", None)
    return jax.shard_map(
        per_device, mesh=mesh, in_specs=in_specs, out_specs=out_specs, check_vma=False
    )
```

```python
import functools

import jax
import jax.numpy as jnp
from jax import lax
from jax.experimental import pallas as pl
from jax.experimental.pallas import tpu as pltpu
from jax.sharding import PartitionSpec as P

HID = 32
SEQS = 64
C_Z = 128
NY, NZ, NX, NC = 2, 8, 4, 2
PACK = 4


def device_index(y, z, x, c):
    return ((y % NY * NZ + z % NZ) * NX + x % NX) * NC + c % NC


def shift(move):
    pairs = []
    for y in range(NY):
        for z in range(NZ):
            for x in range(NX):
                for c in range(NC):
                    pairs.append((device_index(y, z, x, c), device_index(*move(y, z, x, c))))
    return pairs


def side(c):
    return 1 - 2 * c


Z_EVEN = {k: shift(lambda y, z, x, c, k=k: (y, z + k, x, c)) for k in (2, 4, 6)}
Y_PAIR = shift(lambda y, z, x, c: (y + 1, z, x, c))
Z_PAIR = shift(lambda y, z, x, c: (y, z ^ 1, x, c))
YZ_PAIR = shift(lambda y, z, x, c: (y + 1, z ^ 1, x, c))
X_SIDE = shift(lambda y, z, x, c: (y, z, x + side(c), c))
X_BACK = shift(lambda y, z, x, c: (y, z, x - side(c), c))
CORE_PAIR = shift(lambda y, z, x, c: (y, z, x, c + 1))
BACKS = (4, 2, 6)
PARTS = [(t, b, back) for b in range(2) for t in range(NY) for back in (0, *BACKS)]


def cost(flops, bytes_accessed):
    return pl.CostEstimate(flops=flops, bytes_accessed=bytes_accessed, transcendentals=0)


def send(block, pairs):
    return lax.ppermute(block, "dap", pairs)


def join(blocks):
    rows = blocks[0].shape[0]
    whole = jnp.zeros((rows * len(blocks), blocks[0].shape[1]), blocks[0].dtype)
    for k, block in enumerate(blocks):
        whole = lax.dynamic_update_slice(whole, block, (k * rows, 0))
    return whole


def layer_norm(feats, gain, offset):
    values = feats.astype(jnp.float32)
    center = jnp.mean(values, axis=-1, keepdims=True)
    spread = jnp.mean((values - center) ** 2, axis=-1, keepdims=True)
    return (values - center) * lax.rsqrt(spread + 1e-05) * gain + offset


def dot_last(a, b):
    return lax.dot_general(a, b, (((1,), (1,)), ((), ())), preferred_element_type=jnp.float32)


def left_kernel(feats_ref, gain_ref, offset_ref, weight_ref, bias_ref, left_ref):
    groups = SEQS // PACK
    rows = feats_ref.shape[1]
    normed = layer_norm(feats_ref[...], gain_ref[...], offset_ref[...])
    normed = normed.reshape(groups, PACK, rows, -1)
    wide = jnp.concatenate([normed[:, k] for k in range(PACK)], axis=-1)
    wide = wide.reshape(groups * rows, -1).astype(jnp.bfloat16)
    weight = jnp.concatenate([weight_ref[...].astype(jnp.float32)] * PACK, axis=0)
    turn = lax.broadcasted_iota(jnp.int32, weight.shape, 0) // HID
    diagonal = jnp.concatenate(
        [jnp.where(turn == k, weight, 0.0) for k in range(PACK)], axis=1
    ).astype(jnp.bfloat16)
    bias = jnp.concatenate([bias_ref[...]] * PACK, axis=1)
    out = dot_last(wide, diagonal) + bias
    for g in range(groups):
        left_ref[:, g * PACK * HID : (g + 1) * PACK * HID] = out[
            g * rows : (g + 1) * rows
        ].astype(jnp.bfloat16)


def table_kernel(feats_ref, gain_ref, offset_ref, weight_ref, bias_ref, out_weight_ref, table_ref, right_ref):
    rows = feats_ref.shape[1]
    normed = layer_norm(feats_ref[...], gain_ref[...], offset_ref[...])
    normed = normed.reshape(SEQS * rows, -1).astype(jnp.bfloat16)
    right = dot_last(normed, weight_ref[...]) + bias_ref[...]
    right_ref[...] = right.astype(jnp.bfloat16)
    step = 16

    def body(b, carry):
        start = pl.multiple_of(b * step * rows, step * rows)
        part = jnp.dot(
            right_ref[pl.ds(start, step * rows), :],
            out_weight_ref[...],
            preferred_element_type=jnp.float32,
        ) * (1.0 / SEQS)
        part = part.reshape(step * rows, HID, C_Z)
        for s in range(step):
            at = pl.multiple_of((b * step + s) * HID, HID)
            for j in range(rows):
                table_ref[pl.ds(at, HID), j * C_Z : (j + 1) * C_Z] = part[s * rows + j].astype(
                    jnp.bfloat16
                )
        return carry

    lax.fori_loop(0, SEQS // step, body, 0)


def pair_kernel(*refs, pieces, aliased):
    lefts = refs[: len(pieces)]
    table_ref, bias_ref = refs[len(pieces) : len(pieces) + 2]
    out_ref, left_all, acc_ref, ready, sems = refs[len(pieces) + 2 + aliased :]
    rows = lefts[0].shape[0]
    if len(lefts) == 1:
        left_all = lefts[0]
    else:
        for n, left_ref in enumerate(lefts):
            left_all[n * rows : (n + 1) * rows, :] = left_ref[...]
    acc_ref[...] = jnp.dot(left_all[...], table_ref[...], preferred_element_type=jnp.float32)
    me = lax.axis_index("dap")
    core = lax.rem(me, NC)
    x = lax.rem(lax.div(me, NC), NX)
    z = lax.rem(lax.div(me, NC * NX), NZ)
    y = lax.div(me, NC * NX * NZ)
    copies = []
    for n, (lane, ahead) in enumerate(pieces):
        c = core if lane == 0 else 1 - core
        to_x = lax.rem(x + ahead * side(core) + NX, NX)
        count = rows // 8
        first = n * count % len(PARTS)
        for k, (t, b, back) in enumerate(PARTS[first : first + count]):
            slot = n * count + k
            part = acc_ref[slot * 8 : slot * 8 + 8, :].reshape(8, 8, C_Z) + bias_ref[...]
            ready[slot] = part.astype(jnp.bfloat16)
            to_y = lax.rem(y + t, NY)
            to_z = lax.rem((z + b * (1 - 2 * lax.rem(z, 2))) - back + NZ, NZ)
            to = ((to_y * NZ + to_z) * NX + to_x) * NC + c
            copy = pltpu.make_async_copy(ready.at[slot], out_ref.at[to], sems.at[slot])
            copy.start()
            copies.append(copy)
    for copy in copies:
        copy.wait()


def pair_block(lefts, pieces, table, bias, out, reach=10 << 20):
    aliased = out is not None
    vmem, anywhere = pl.BlockSpec(memory_space=pltpu.VMEM), pl.BlockSpec(memory_space=pl.ANY)
    operands = [*lefts, table, bias] + ([out] if aliased else [])
    rows = sum(left.shape[0] for left in lefts)
    depth, width = table.shape
    blocks = rows // 8
    return pl.pallas_call(
        functools.partial(pair_kernel, pieces=pieces, aliased=int(aliased)),
        in_specs=[vmem] * (len(lefts) + 2) + ([anywhere] if aliased else []),
        out_specs=anywhere,
        out_shape=jax.ShapeDtypeStruct((NY * NZ * NX * NC, 8, 8, C_Z), jnp.bfloat16),
        scratch_shapes=[
            pltpu.VMEM((rows, depth), jnp.bfloat16),
            pltpu.VMEM((rows, width), jnp.float32),
            pltpu.VMEM((blocks, 8, 8, C_Z), jnp.bfloat16),
            pltpu.SemaphoreType.DMA((blocks,)),
        ],
        input_output_aliases={len(operands) - 1: 0} if aliased else {},
        compiler_params=pltpu.CompilerParams(vmem_limit_bytes=24 * 1024 * 1024),
        cost_estimate=cost(2 * rows * depth * width, reach),
    )(*operands)


def per_device(
    alignment_features,
    layer_norm_gain,
    layer_norm_bias,
    left_projection_weight,
    left_projection_bias,
    right_projection_weight,
    right_projection_bias,
    output_weight,
    output_bias,
):
    rows = alignment_features.shape[1]
    gain, offset = layer_norm_gain[None], layer_norm_bias[None]
    vmem = pltpu.CompilerParams(vmem_limit_bytes=32 * 1024 * 1024)
    left = pl.pallas_call(
        left_kernel,
        out_shape=pltpu.VMEM((rows, SEQS * HID), jnp.bfloat16),
        out_specs=pl.BlockSpec(memory_space=pltpu.VMEM),
        compiler_params=pltpu.CompilerParams(vmem_limit_bytes=60 * 1024 * 1024),
    )(
        alignment_features,
        gain,
        offset,
        left_projection_weight.T,
        left_projection_bias[None],
    )
    out_weight = output_weight.reshape(HID, HID, C_Z).transpose(1, 0, 2).reshape(HID, HID * C_Z)
    table = pl.pallas_call(
        table_kernel,
        out_shape=jax.ShapeDtypeStruct((SEQS * HID, rows * C_Z), jnp.bfloat16),
        scratch_shapes=[pltpu.VMEM((SEQS * rows, HID), jnp.bfloat16)],
        compiler_params=vmem,
        cost_estimate=cost(1 << 30, 24 << 20),
    )(
        alignment_features,
        gain,
        offset,
        right_projection_weight.T,
        right_projection_bias[None],
        out_weight,
    )

    bias = output_bias[None]

    ring = join([left] + [send(left, Z_EVEN[k]) for k in BACKS])
    block = join([ring, send(ring, Y_PAIR), send(ring, Z_PAIR), send(ring, YZ_PAIR)])
    ahead, behind = send(block, X_BACK), send(block, X_SIDE)
    half = block.shape[0] // 2
    parts = [block[:half], block[half:]]
    parts += [send(part, CORE_PAIR) for part in parts]
    out = pair_block(parts, [(0, 0), (0, 0), (1, 0), (1, 0)], table, bias, None)
    ahead, behind, table, out = lax.optimization_barrier((ahead, behind, table, out))
    far = send(behind, X_SIDE)
    out = pair_block([ahead, behind], [(0, 1), (0, -1)], table, bias, out, 100 << 20)
    ahead, behind, out = lax.optimization_barrier((ahead, behind, out))
    others = [send(part, CORE_PAIR) for b in (ahead, behind) for part in (b[:half], b[half:])]
    out = pair_block(others, [(1, -1), (1, -1), (1, 1), (1, 1)], table, bias, out, 1 << 10)
    far, out = lax.optimization_barrier((far, out))
    far_other = send(far, CORE_PAIR)
    out = pair_block([far], [(0, 2)], table, bias, out)
    out = pair_block([far_other], [(1, 2)], table, bias, out)
    return out.reshape(NY * NZ * NX * NC * 8, 8, C_Z)


def solution(mesh):
    in_specs = (P(None, ("dp", "dap"), None), P(), P(), P(), P(), P(), P(), P(), P())
    out_specs = P("dp", "dap", None)
    return jax.shard_map(
        per_device, mesh=mesh, in_specs=in_specs, out_specs=out_specs, check_vma=False
    )
```

```python
import functools

import jax
import jax.numpy as jnp
from jax import lax
from jax.experimental import pallas as pl
from jax.experimental.pallas import tpu as pltpu
from jax.sharding import PartitionSpec as P

HID = 32
SEQS = 64
C_Z = 128
NY, NZ, NX, NC = 2, 8, 4, 2
PACK = 4


def device_index(y, z, x, c):
    return ((y % NY * NZ + z % NZ) * NX + x % NX) * NC + c % NC


def shift(move):
    pairs = []
    for y in range(NY):
        for z in range(NZ):
            for x in range(NX):
                for c in range(NC):
                    pairs.append((device_index(y, z, x, c), device_index(*move(y, z, x, c))))
    return pairs


def side(c):
    return 1 - 2 * c


Z_EVEN = {k: shift(lambda y, z, x, c, k=k: (y, z + k, x, c)) for k in (2, 4, 6)}
Y_PAIR = shift(lambda y, z, x, c: (y + 1, z, x, c))
Z_PAIR = shift(lambda y, z, x, c: (y, z ^ 1, x, c))
YZ_PAIR = shift(lambda y, z, x, c: (y + 1, z ^ 1, x, c))
X_SIDE = shift(lambda y, z, x, c: (y, z, x + side(c), c))
X_BACK = shift(lambda y, z, x, c: (y, z, x - side(c), c))
CORE_PAIR = shift(lambda y, z, x, c: (y, z, x, c + 1))
BACKS = (4, 2, 6)
PARTS = [(t, b, back) for b in range(2) for t in range(NY) for back in (0, *BACKS)]


def cost(flops, bytes_accessed):
    return pl.CostEstimate(flops=flops, bytes_accessed=bytes_accessed, transcendentals=0)


def send(block, pairs):
    return lax.ppermute(block, "dap", pairs)


def join(blocks):
    rows = blocks[0].shape[0]
    whole = jnp.zeros((rows * len(blocks), blocks[0].shape[1]), blocks[0].dtype)
    for k, block in enumerate(blocks):
        whole = lax.dynamic_update_slice(whole, block, (k * rows, 0))
    return whole


def layer_norm(feats, gain, offset):
    values = feats.astype(jnp.float32)
    center = jnp.mean(values, axis=-1, keepdims=True)
    spread = jnp.mean((values - center) ** 2, axis=-1, keepdims=True)
    return (values - center) * lax.rsqrt(spread + 1e-05) * gain + offset


def dot_last(a, b):
    return lax.dot_general(a, b, (((1,), (1,)), ((), ())), preferred_element_type=jnp.float32)


def left_kernel(feats_ref, gain_ref, offset_ref, weight_ref, bias_ref, left_ref):
    groups = SEQS // PACK
    rows = feats_ref.shape[1]
    normed = layer_norm(feats_ref[...], gain_ref[...], offset_ref[...])
    normed = normed.reshape(groups, PACK, rows, -1)
    wide = jnp.concatenate([normed[:, k] for k in range(PACK)], axis=-1)
    wide = wide.reshape(groups * rows, -1).astype(jnp.bfloat16)
    weight = jnp.concatenate([weight_ref[...].astype(jnp.float32)] * PACK, axis=0)
    turn = lax.broadcasted_iota(jnp.int32, weight.shape, 0) // HID
    diagonal = jnp.concatenate(
        [jnp.where(turn == k, weight, 0.0) for k in range(PACK)], axis=1
    ).astype(jnp.bfloat16)
    bias = jnp.concatenate([bias_ref[...]] * PACK, axis=1)
    out = dot_last(wide, diagonal) + bias
    for g in range(groups):
        left_ref[:, g * PACK * HID : (g + 1) * PACK * HID] = out[
            g * rows : (g + 1) * rows
        ].astype(jnp.bfloat16)


def table_kernel(feats_ref, gain_ref, offset_ref, weight_ref, bias_ref, out_weight_ref, table_ref, right_ref):
    rows = feats_ref.shape[1]
    normed = layer_norm(feats_ref[...], gain_ref[...], offset_ref[...])
    normed = normed.reshape(SEQS * rows, -1).astype(jnp.bfloat16)
    right = dot_last(normed, weight_ref[...]) + bias_ref[...]
    right_ref[...] = right.astype(jnp.bfloat16)
    step = 16

    def body(b, carry):
        start = pl.multiple_of(b * step * rows, step * rows)
        part = jnp.dot(
            right_ref[pl.ds(start, step * rows), :],
            out_weight_ref[...],
            preferred_element_type=jnp.float32,
        ) * (1.0 / SEQS)
        part = part.reshape(step * rows, HID, C_Z)
        for s in range(step):
            at = pl.multiple_of((b * step + s) * HID, HID)
            for j in range(rows):
                table_ref[pl.ds(at, HID), j * C_Z : (j + 1) * C_Z] = part[s * rows + j].astype(
                    jnp.bfloat16
                )
        return carry

    lax.fori_loop(0, SEQS // step, body, 0)


def pair_kernel(*refs, pieces, aliased):
    lefts = refs[: len(pieces)]
    table_ref, bias_ref = refs[len(pieces) : len(pieces) + 2]
    out_ref, left_all, acc_ref, ready, sems = refs[len(pieces) + 2 + aliased :]
    rows = lefts[0].shape[0]
    if len(lefts) == 1:
        left_all = lefts[0]
    else:
        for n, left_ref in enumerate(lefts):
            left_all[n * rows : (n + 1) * rows, :] = left_ref[...]
    acc_ref[...] = jnp.dot(left_all[...], table_ref[...], preferred_element_type=jnp.float32)
    me = lax.axis_index("dap")
    core = lax.rem(me, NC)
    x = lax.rem(lax.div(me, NC), NX)
    z = lax.rem(lax.div(me, NC * NX), NZ)
    y = lax.div(me, NC * NX * NZ)
    copies = []
    for n, (lane, ahead) in enumerate(pieces):
        c = core if lane == 0 else 1 - core
        to_x = lax.rem(x + ahead * side(core) + NX, NX)
        count = rows // 8
        first = n * count % len(PARTS)
        for k, (t, b, back) in enumerate(PARTS[first : first + count]):
            slot = n * count + k
            part = acc_ref[slot * 8 : slot * 8 + 8, :].reshape(8, 8, C_Z) + bias_ref[...]
            ready[slot] = part.astype(jnp.bfloat16)
            to_y = lax.rem(y + t, NY)
            to_z = lax.rem((z + b * (1 - 2 * lax.rem(z, 2))) - back + NZ, NZ)
            to = ((to_y * NZ + to_z) * NX + to_x) * NC + c
            copy = pltpu.make_async_copy(ready.at[slot], out_ref.at[to], sems.at[slot])
            copy.start()
            copies.append(copy)
    for copy in copies:
        copy.wait()


def pair_block(lefts, pieces, table, bias, out, reach=10 << 20):
    aliased = out is not None
    vmem, anywhere = pl.BlockSpec(memory_space=pltpu.VMEM), pl.BlockSpec(memory_space=pl.ANY)
    operands = [*lefts, table, bias] + ([out] if aliased else [])
    rows = sum(left.shape[0] for left in lefts)
    depth, width = table.shape
    blocks = rows // 8
    return pl.pallas_call(
        functools.partial(pair_kernel, pieces=pieces, aliased=int(aliased)),
        in_specs=[vmem] * (len(lefts) + 2) + ([anywhere] if aliased else []),
        out_specs=anywhere,
        out_shape=jax.ShapeDtypeStruct((NY * NZ * NX * NC, 8, 8, C_Z), jnp.bfloat16),
        scratch_shapes=[
            pltpu.VMEM((rows, depth), jnp.bfloat16),
            pltpu.VMEM((rows, width), jnp.float32),
            pltpu.VMEM((blocks, 8, 8, C_Z), jnp.bfloat16),
            pltpu.SemaphoreType.DMA((blocks,)),
        ],
        input_output_aliases={len(operands) - 1: 0} if aliased else {},
        compiler_params=pltpu.CompilerParams(vmem_limit_bytes=24 * 1024 * 1024),
        cost_estimate=cost(2 * rows * depth * width, reach),
    )(*operands)


def per_device(
    alignment_features,
    layer_norm_gain,
    layer_norm_bias,
    left_projection_weight,
    left_projection_bias,
    right_projection_weight,
    right_projection_bias,
    output_weight,
    output_bias,
):
    rows = alignment_features.shape[1]
    gain, offset = layer_norm_gain[None], layer_norm_bias[None]
    vmem = pltpu.CompilerParams(vmem_limit_bytes=32 * 1024 * 1024)
    left = pl.pallas_call(
        left_kernel,
        out_shape=pltpu.VMEM((rows, SEQS * HID), jnp.bfloat16),
        out_specs=pl.BlockSpec(memory_space=pltpu.VMEM),
        compiler_params=pltpu.CompilerParams(vmem_limit_bytes=60 * 1024 * 1024),
    )(
        alignment_features,
        gain,
        offset,
        left_projection_weight.T,
        left_projection_bias[None],
    )
    out_weight = output_weight.reshape(HID, HID, C_Z).transpose(1, 0, 2).reshape(HID, HID * C_Z)
    table = pl.pallas_call(
        table_kernel,
        out_shape=jax.ShapeDtypeStruct((SEQS * HID, rows * C_Z), jnp.bfloat16),
        scratch_shapes=[pltpu.VMEM((SEQS * rows, HID), jnp.bfloat16)],
        compiler_params=vmem,
        cost_estimate=cost(1 << 30, 24 << 20),
    )(
        alignment_features,
        gain,
        offset,
        right_projection_weight.T,
        right_projection_bias[None],
        out_weight,
    )

    bias = output_bias[None]

    ring = join([left] + [send(left, Z_EVEN[k]) for k in BACKS])
    block = join([ring, send(ring, Y_PAIR), send(ring, Z_PAIR), send(ring, YZ_PAIR)])
    ahead, behind = send(block, X_BACK), send(block, X_SIDE)
    half = block.shape[0] // 2
    parts = [block[:half], block[half:]]
    parts += [send(part, CORE_PAIR) for part in parts]
    out = pair_block(parts, [(0, 0), (0, 0), (1, 0), (1, 0)], table, bias, None)
    behind, table, out = lax.optimization_barrier((behind, table, out))
    far = send(behind, X_SIDE)
    out = pair_block([ahead, behind], [(0, 1), (0, -1)], table, bias, out, 100 << 20)
    ahead, behind, out = lax.optimization_barrier((ahead, behind, out))
    others = [send(part, CORE_PAIR) for b in (ahead, behind) for part in (b[:half], b[half:])]
    out = pair_block(others, [(1, -1), (1, -1), (1, 1), (1, 1)], table, bias, out, 1 << 10)
    far, out = lax.optimization_barrier((far, out))
    far_other = send(far, CORE_PAIR)
    out = pair_block([far], [(0, 2)], table, bias, out)
    out = pair_block([far_other], [(1, 2)], table, bias, out)
    return out.reshape(NY * NZ * NX * NC * 8, 8, C_Z)


def solution(mesh):
    in_specs = (P(None, ("dp", "dap"), None), P(), P(), P(), P(), P(), P(), P(), P())
    out_specs = P("dp", "dap", None)
    return jax.shard_map(
        per_device, mesh=mesh, in_specs=in_specs, out_specs=out_specs, check_vma=False
    )
```

```python
import functools

import jax
import jax.numpy as jnp
from jax import lax
from jax.experimental import pallas as pl
from jax.experimental.pallas import tpu as pltpu
from jax.sharding import PartitionSpec as P

HID = 32
SEQS = 64
C_Z = 128
NY, NZ, NX, NC = 2, 8, 4, 2
PACK = 4


def device_index(y, z, x, c):
    return ((y % NY * NZ + z % NZ) * NX + x % NX) * NC + c % NC


def shift(move):
    pairs = []
    for y in range(NY):
        for z in range(NZ):
            for x in range(NX):
                for c in range(NC):
                    pairs.append((device_index(y, z, x, c), device_index(*move(y, z, x, c))))
    return pairs


def side(c):
    return 1 - 2 * c


Z_EVEN = {k: shift(lambda y, z, x, c, k=k: (y, z + k, x, c)) for k in (2, 4, 6)}
Y_PAIR = shift(lambda y, z, x, c: (y + 1, z, x, c))
Z_PAIR = shift(lambda y, z, x, c: (y, z ^ 1, x, c))
YZ_PAIR = shift(lambda y, z, x, c: (y + 1, z ^ 1, x, c))
X_SIDE = shift(lambda y, z, x, c: (y, z, x + side(c), c))
X_BACK = shift(lambda y, z, x, c: (y, z, x - side(c), c))
CORE_PAIR = shift(lambda y, z, x, c: (y, z, x, c + 1))
BACKS = (4, 2, 6)
PARTS = [(t, b, back) for b in range(2) for t in range(NY) for back in (0, *BACKS)]


def cost(flops, bytes_accessed):
    return pl.CostEstimate(flops=flops, bytes_accessed=bytes_accessed, transcendentals=0)


def send(block, pairs):
    return lax.ppermute(block, "dap", pairs)


def join(blocks):
    rows = blocks[0].shape[0]
    whole = jnp.zeros((rows * len(blocks), blocks[0].shape[1]), blocks[0].dtype)
    for k, block in enumerate(blocks):
        whole = lax.dynamic_update_slice(whole, block, (k * rows, 0))
    return whole


def layer_norm(feats, gain, offset):
    values = feats.astype(jnp.float32)
    center = jnp.mean(values, axis=-1, keepdims=True)
    spread = jnp.mean((values - center) ** 2, axis=-1, keepdims=True)
    return (values - center) * lax.rsqrt(spread + 1e-05) * gain + offset


def dot_last(a, b):
    return lax.dot_general(a, b, (((1,), (1,)), ((), ())), preferred_element_type=jnp.float32)


def left_kernel(feats_ref, gain_ref, offset_ref, weight_ref, bias_ref, left_ref):
    groups = SEQS // PACK
    rows = feats_ref.shape[1]
    normed = layer_norm(feats_ref[...], gain_ref[...], offset_ref[...])
    normed = normed.reshape(groups, PACK, rows, -1)
    wide = jnp.concatenate([normed[:, k] for k in range(PACK)], axis=-1)
    wide = wide.reshape(groups * rows, -1).astype(jnp.bfloat16)
    weight = jnp.concatenate([weight_ref[...].astype(jnp.float32)] * PACK, axis=0)
    turn = lax.broadcasted_iota(jnp.int32, weight.shape, 0) // HID
    diagonal = jnp.concatenate(
        [jnp.where(turn == k, weight, 0.0) for k in range(PACK)], axis=1
    ).astype(jnp.bfloat16)
    bias = jnp.concatenate([bias_ref[...]] * PACK, axis=1)
    out = dot_last(wide, diagonal) + bias
    for g in range(groups):
        left_ref[:, g * PACK * HID : (g + 1) * PACK * HID] = out[
            g * rows : (g + 1) * rows
        ].astype(jnp.bfloat16)


def table_kernel(feats_ref, gain_ref, offset_ref, weight_ref, bias_ref, out_weight_ref, table_ref, right_ref):
    rows = feats_ref.shape[1]
    normed = layer_norm(feats_ref[...], gain_ref[...], offset_ref[...])
    normed = normed.reshape(SEQS * rows, -1).astype(jnp.bfloat16)
    right = dot_last(normed, weight_ref[...]) + bias_ref[...]
    right_ref[...] = right.astype(jnp.bfloat16)
    step = 16

    def body(b, carry):
        start = pl.multiple_of(b * step * rows, step * rows)
        part = jnp.dot(
            right_ref[pl.ds(start, step * rows), :],
            out_weight_ref[...],
            preferred_element_type=jnp.float32,
        ) * (1.0 / SEQS)
        part = part.reshape(step * rows, HID, C_Z)
        for s in range(step):
            at = pl.multiple_of((b * step + s) * HID, HID)
            for j in range(rows):
                table_ref[pl.ds(at, HID), j * C_Z : (j + 1) * C_Z] = part[s * rows + j].astype(
                    jnp.bfloat16
                )
        return carry

    lax.fori_loop(0, SEQS // step, body, 0)


def pair_kernel(*refs, pieces, aliased):
    lefts = refs[: len(pieces)]
    table_ref, bias_ref = refs[len(pieces) : len(pieces) + 2]
    out_ref, left_all, acc_ref, ready, sems = refs[len(pieces) + 2 + aliased :]
    rows = lefts[0].shape[0]
    if len(lefts) == 1:
        left_all = lefts[0]
    else:
        for n, left_ref in enumerate(lefts):
            left_all[n * rows : (n + 1) * rows, :] = left_ref[...]
    bias = jnp.concatenate([bias_ref[...]] * 8, axis=1)
    acc_ref[...] = jnp.dot(left_all[...], table_ref[...], preferred_element_type=jnp.float32) + bias
    me = lax.axis_index("dap")
    core = lax.rem(me, NC)
    x = lax.rem(lax.div(me, NC), NX)
    z = lax.rem(lax.div(me, NC * NX), NZ)
    y = lax.div(me, NC * NX * NZ)
    copies = []
    for n, (lane, ahead) in enumerate(pieces):
        c = core if lane == 0 else 1 - core
        to_x = lax.rem(x + ahead * side(core) + NX, NX)
        count = rows // 8
        first = n * count % len(PARTS)
        for k, (t, b, back) in enumerate(PARTS[first : first + count]):
            slot = n * count + k
            part = acc_ref[slot * 8 : slot * 8 + 8, :].reshape(8, 8, C_Z)
            ready[slot] = part.astype(jnp.bfloat16)
            to_y = lax.rem(y + t, NY)
            to_z = lax.rem((z + b * (1 - 2 * lax.rem(z, 2))) - back + NZ, NZ)
            to = ((to_y * NZ + to_z) * NX + to_x) * NC + c
            copy = pltpu.make_async_copy(ready.at[slot], out_ref.at[to], sems.at[slot])
            copy.start()
            copies.append(copy)
    for copy in copies:
        copy.wait()


def pair_block(lefts, pieces, table, bias, out, reach=10 << 20):
    aliased = out is not None
    vmem, anywhere = pl.BlockSpec(memory_space=pltpu.VMEM), pl.BlockSpec(memory_space=pl.ANY)
    operands = [*lefts, table, bias] + ([out] if aliased else [])
    rows = sum(left.shape[0] for left in lefts)
    depth, width = table.shape
    blocks = rows // 8
    return pl.pallas_call(
        functools.partial(pair_kernel, pieces=pieces, aliased=int(aliased)),
        in_specs=[vmem] * (len(lefts) + 2) + ([anywhere] if aliased else []),
        out_specs=anywhere,
        out_shape=jax.ShapeDtypeStruct((NY * NZ * NX * NC, 8, 8, C_Z), jnp.bfloat16),
        scratch_shapes=[
            pltpu.VMEM((rows, depth), jnp.bfloat16),
            pltpu.VMEM((rows, width), jnp.float32),
            pltpu.VMEM((blocks, 8, 8, C_Z), jnp.bfloat16),
            pltpu.SemaphoreType.DMA((blocks,)),
        ],
        input_output_aliases={len(operands) - 1: 0} if aliased else {},
        compiler_params=pltpu.CompilerParams(vmem_limit_bytes=24 * 1024 * 1024),
        cost_estimate=cost(2 * rows * depth * width, reach),
    )(*operands)


def per_device(
    alignment_features,
    layer_norm_gain,
    layer_norm_bias,
    left_projection_weight,
    left_projection_bias,
    right_projection_weight,
    right_projection_bias,
    output_weight,
    output_bias,
):
    rows = alignment_features.shape[1]
    gain, offset = layer_norm_gain[None], layer_norm_bias[None]
    vmem = pltpu.CompilerParams(vmem_limit_bytes=32 * 1024 * 1024)
    left = pl.pallas_call(
        left_kernel,
        out_shape=pltpu.VMEM((rows, SEQS * HID), jnp.bfloat16),
        out_specs=pl.BlockSpec(memory_space=pltpu.VMEM),
        compiler_params=pltpu.CompilerParams(vmem_limit_bytes=60 * 1024 * 1024),
    )(
        alignment_features,
        gain,
        offset,
        left_projection_weight.T,
        left_projection_bias[None],
    )
    out_weight = output_weight.reshape(HID, HID, C_Z).transpose(1, 0, 2).reshape(HID, HID * C_Z)
    table = pl.pallas_call(
        table_kernel,
        out_shape=jax.ShapeDtypeStruct((SEQS * HID, rows * C_Z), jnp.bfloat16),
        scratch_shapes=[pltpu.VMEM((SEQS * rows, HID), jnp.bfloat16)],
        compiler_params=vmem,
        cost_estimate=cost(1 << 30, 24 << 20),
    )(
        alignment_features,
        gain,
        offset,
        right_projection_weight.T,
        right_projection_bias[None],
        out_weight,
    )

    bias = output_bias[None]

    ring = join([left] + [send(left, Z_EVEN[k]) for k in BACKS])
    block = join([ring, send(ring, Y_PAIR), send(ring, Z_PAIR), send(ring, YZ_PAIR)])
    ahead, behind = send(block, X_BACK), send(block, X_SIDE)
    half = block.shape[0] // 2
    parts = [block[:half], block[half:]]
    parts += [send(part, CORE_PAIR) for part in parts]
    out = pair_block(parts, [(0, 0), (0, 0), (1, 0), (1, 0)], table, bias, None)
    behind, table, out = lax.optimization_barrier((behind, table, out))
    far = send(behind, X_SIDE)
    out = pair_block([ahead, behind], [(0, 1), (0, -1)], table, bias, out, 100 << 20)
    ahead, behind, out = lax.optimization_barrier((ahead, behind, out))
    others = [send(part, CORE_PAIR) for b in (ahead, behind) for part in (b[:half], b[half:])]
    out = pair_block(others, [(1, -1), (1, -1), (1, 1), (1, 1)], table, bias, out, 1 << 10)
    far, out = lax.optimization_barrier((far, out))
    far_other = send(far, CORE_PAIR)
    out = pair_block([far], [(0, 2)], table, bias, out)
    out = pair_block([far_other], [(1, 2)], table, bias, out)
    return out.reshape(NY * NZ * NX * NC * 8, 8, C_Z)


def solution(mesh):
    in_specs = (P(None, ("dp", "dap"), None), P(), P(), P(), P(), P(), P(), P(), P())
    out_specs = P("dp", "dap", None)
    return jax.shard_map(
        per_device, mesh=mesh, in_specs=in_specs, out_specs=out_specs, check_vma=False
    )
```
